32 devices in a mesh: sector: 8 (over z, x), tile: 4 (over y, core).
Axes of the slice: x: 2, y: 2, z: 4, core: 2. Of those that a mesh axis runs over, the one named last changes fastest.
Arguments:
- rates: bfloat16 [16384, 1024], P(('sector', 'tile')), may hold values from -6 to 6
- target: bfloat16 [16384, 1024], P(('sector', 'tile')), may hold values from -6 to 6
- prior_consensus: float32 [16384, 1024], P(('sector', 'tile')), may hold values from -6 to 6
- duals: float32 [16384, 1024], P(('sector', 'tile')), may hold values from -6 to 6
- response: bfloat16 [16384, 512], P(('sector', 'tile')), may hold values from -0.25 to 0.25
- block_cols: int32 [128, 4], P(('sector', 'tile')), may hold values from 0 to 15, all different within a row
- slot_well: int32 [16384], P(('sector', 'tile')), may hold values from -1 to 1535, as said below
- well_owner: int32 [1536], replicated, may hold values from 0 to 31, as said below
Outputs:
- new_rates: bfloat16 [16384, 1024], P(('sector', 'tile'))
- new_duals: float32 [16384, 1024], P(('sector', 'tile'))
- consensus: float32 [16384, 1024], P(('sector', 'tile'))
The draws below stay inside these ranges and needn't reach their ends.
Inputs may be any that keep to these rules, and one draw needn't show every extreme that they name: `block_cols`: each row names 4 different column blocks. `well_owner`: each device owns exactly 48 wells. `slot_well`: every well has exactly one slot on its owner device and at most one slot in each other sector, always on a device with the owner's tile index. The slots of one device holding wells owned in one other sector number at most 4; in every draw each device reaches 4 toward some sector, and some sector receives 4 from every other sector of each tile index.
All inputs are finite; a program needn't handle non-finite values.
Results may differ from the reference program's by a relative error of at most 0.0044.
Values may be sent and summed in bfloat16 or wider, within the bound.
A program may use at most 128 MiB of HBM per device.

```python
import jax
import jax.numpy as jnp
from jax import lax

SLOT_DEV = 512
PER = 1024
NB = 4
INNER = 3
OWN = 48
CAP = 4
SLOTS = 16384
WELLS = 1536
SEC_BLKS = 16
ROWBLKS = 128
N_SECTOR = 8
N_TILE = 4


def common_layout(key):
    base = jax.random.fold_in(key, 7301)
    subkeys = jax.random.split(base, 6)
    sector_count = N_SECTOR
    tile_count = N_TILE
    device_count = sector_count * tile_count
    shuffled = jax.random.permutation(subkeys[0], WELLS).astype(jnp.int32)
    owners = (jnp.arange(WELLS) // OWN).astype(jnp.int32)
    well_owner = jnp.zeros((WELLS,), jnp.int32).at[shuffled].set(owners)
    owned_ids = shuffled.reshape(sector_count, tile_count, OWN)
    sector_limit = 1 + jax.random.randint(subkeys[1], (sector_count,), 0, CAP)
    shape3 = (tile_count, sector_count, sector_count)
    lower_bound = jnp.broadcast_to((sector_limit // 2)[None, :, None], shape3)
    upper_bound = jnp.broadcast_to((sector_limit + 1)[None, :, None], shape3)
    counts = jax.random.randint(subkeys[2], shape3, lower_bound, upper_bound)
    source = jnp.arange(sector_count)
    destination = jnp.arange(sector_count)
    following = (source + 1) % sector_count
    crowded = jax.random.randint(subkeys[3], (tile_count,), 0, sector_count)
    forced = (destination[None, None, :] == following[None, :, None]) | (destination[None, None, :] == crowded[:, None, None])
    counts = jnp.where(forced, CAP, counts)
    counts = jnp.where(source[None, :, None] == destination[None, None, :], 0, counts)
    pair_keys = jax.random.split(subkeys[4], tile_count * sector_count * sector_count)
    chosen = jax.vmap(lambda subkey: jax.random.permutation(subkey, OWN)[:CAP])(pair_keys)
    chosen = chosen.astype(jnp.int32).reshape(tile_count, sector_count, sector_count, CAP)
    by_tile = jnp.transpose(owned_ids, (1, 0, 2))
    spread = jnp.broadcast_to(by_tile[:, None, :, :], (tile_count, sector_count, sector_count, OWN))
    foreign = jnp.take_along_axis(spread, chosen, axis=3)
    used_slot = jnp.arange(CAP)[None, None, None, :] < counts[:, :, :, None]
    foreign = jnp.where(used_slot, foreign, -1)
    foreign = jnp.transpose(foreign, (1, 0, 2, 3)).reshape(sector_count, tile_count, sector_count * CAP)
    padding = -jnp.ones((sector_count, tile_count, SLOT_DEV - OWN - sector_count * CAP), jnp.int32)
    layout = jnp.concatenate([owned_ids, foreign.astype(jnp.int32), padding], axis=2).reshape(device_count, SLOT_DEV)
    slot_keys = jax.random.split(subkeys[5], device_count)
    mixing = jax.vmap(lambda subkey: jax.random.permutation(subkey, SLOT_DEV))(slot_keys).astype(jnp.int32)
    slot_well = jnp.take_along_axis(layout, mixing, axis=1).reshape(device_count * SLOT_DEV)
    return (slot_well.astype(jnp.int32), well_owner)


def draw_slot_well(key, part):
    return common_layout(key)[0]


def draw_well_owner(key, part):
    return common_layout(key)[1]


def steps_of(key, extent, cuts, low, high):
    def one(dim, shards_of):
        heights = jax.random.uniform(jax.random.fold_in(jax.random.fold_in(key, 6), dim), (shards_of,), jnp.float32, low / len(cuts), high / len(cuts))
        return jnp.repeat(jnp.exp(heights), extent[dim] // shards_of).reshape((-1,) + (1,) * (len(extent) - dim - 1))

    factor_of = one(*cuts[0])
    for cut in cuts[1:]:
        factor_of = factor_of * one(*cut)
    return factor_of


def choose_distinct(rng, rows, amount, top, lift):
    order = jax.random.permutation(jax.random.fold_in(rng, 1), amount)
    boost = order
    for power in range(3):
        boost = boost * boost // amount
    boost = boost * lift // amount
    lots = jax.random.randint(jax.random.fold_in(rng, 2), (rows, amount), 0, 4096) + boost
    holders = jax.random.permutation(jax.random.fold_in(rng, 3), rows)[jnp.arange(amount) % rows]
    lots = jnp.where(jnp.arange(rows)[:, None] == holders[None, :], 1 << 14, lots)
    score = lots * amount + jnp.arange(amount)
    return lax.top_k(score.astype(jnp.int32), top)[1].astype(jnp.int32)


def normal_values(key, shape, scale, limit, cuts=(), held_as=jnp.bfloat16):
    values = jax.random.normal(key, shape, jnp.float32) * scale
    if len(cuts) > 0:
        values = steps_of(key, shape, cuts, -0.22, 0.18) * values
    return jnp.clip(values, min=-limit, max=limit).astype(held_as)


def setup_inputs(seed: int = 0) -> dict:
    arg_keys = jax.random.split(jax.random.key(seed), 9)
    rates = normal_values(arg_keys[0], (SLOTS, PER), 1.0, 6.0, ((0, 32),))
    target = normal_values(arg_keys[1], (SLOTS, PER), 1.0, 6.0, ((0, 32),))
    prior_consensus = normal_values(arg_keys[2], (SLOTS, PER), 1.0, 6.0, ((0, 32),), jnp.float32)
    duals = normal_values(arg_keys[3], (SLOTS, PER), 1.0, 6.0, ((0, 32),), jnp.float32)
    response = normal_values(arg_keys[4], (SLOTS, NB * 128), (NB * 128) ** -0.5, 0.25, ((0, 32),))
    block_cols = choose_distinct(arg_keys[5], ROWBLKS, SEC_BLKS, NB, 0)
    slot_well = draw_slot_well(jax.random.fold_in(arg_keys[8], 71), 0)
    well_owner = draw_well_owner(jax.random.fold_in(arg_keys[8], 71), 0)
    return {"rates": rates, "target": target, "prior_consensus": prior_consensus, "duals": duals, "response": response, "block_cols": block_cols, "slot_well": slot_well, "well_owner": well_owner}


def sector_response(operands):
    sector_rows, coefficients, columns = operands
    periods = sector_rows.shape[1]
    blocks = sector_rows.reshape(SEC_BLKS, 128, periods).astype(jnp.float32)
    picked = blocks[columns.astype(jnp.int32)]
    weights = coefficients.reshape(SEC_BLKS, 128, NB, 128).astype(jnp.float32)
    result = jnp.einsum('bikj,bkjp->bip', weights, picked)
    return result.reshape(SEC_BLKS * 128, periods)


def reference(rates, target, prior_consensus, duals, response, block_cols, slot_well, well_owner):
    periods = rates.shape[1]
    sector_len = N_TILE * SLOT_DEV
    coefficients = response.reshape(N_SECTOR, sector_len, NB * 128)
    columns = block_cols.reshape(N_SECTOR, SEC_BLKS, NB)
    pulled = 0.5 * (prior_consensus - duals)
    iterate = rates
    for iteration in range(INNER):
        drawdown = lax.map(sector_response, (iterate.reshape(N_SECTOR, sector_len, periods), coefficients, columns))
        drawdown = drawdown.reshape(SLOTS, periods)
        iterate = ((iterate.astype(jnp.float32) + 0.5 * (target.astype(jnp.float32) - drawdown) + pulled) / 1.5).astype(jnp.bfloat16)
    new_rates = iterate
    rates_wide = new_rates.astype(jnp.float32)
    offered = lax.optimization_barrier((rates_wide + duals).astype(jnp.bfloat16)).astype(jnp.float32)
    shared = slot_well >= 0
    well_ids = jnp.clip(slot_well, 0, WELLS - 1).astype(jnp.int32)
    device_of = (jnp.arange(SLOTS) // SLOT_DEV).astype(jnp.int32)
    home_slot = shared & (well_owner[well_ids] == device_of)
    weight = jnp.where(shared, jnp.where(home_slot, 2.0, 1.0), 0.0).astype(jnp.float32)
    segment = jnp.where(shared, well_ids, WELLS).astype(jnp.int32)
    totals = jax.ops.segment_sum(offered * weight[:, None], segment, num_segments=WELLS + 1)
    weight_sum = jax.ops.segment_sum(weight, segment, num_segments=WELLS + 1)
    mean_rate = totals[:WELLS] / weight_sum[:WELLS, None]
    consensus = jnp.where(shared[:, None], mean_rate[well_ids], rates_wide)
    new_duals = jnp.where(shared[:, None], duals + rates_wide - consensus, duals)
    return new_rates, new_duals, consensus
```

```python
import jax
import jax.numpy as jnp
from jax import lax
from jax.experimental import pallas as pl
from jax.experimental.pallas import tpu as pltpu
from jax.sharding import PartitionSpec as P

NB = 4
INNER = 3
CAP = 4
BLK = 128


def steps_kernel(cols_ref, mixed_ref, coef_ref, out_ref, state, picked):
    row_blocks = out_ref.shape[0] // BLK
    for step in range(INNER):
        source = mixed_ref.at[0] if step == 0 else state.at[(step + 1) % 2]
        target = out_ref if step == INNER - 1 else state.at[step % 2]

        @pl.loop(0, row_blocks)
        def _(block):
            rows = pl.ds(pl.multiple_of(block * BLK, BLK), BLK)
            for n in range(NB):
                at = pl.multiple_of(cols_ref[block * NB + n] * BLK, BLK)
                picked[n * BLK : (n + 1) * BLK, :] = source[pl.ds(at, BLK), :]
            drawdown = jnp.dot(coef_ref[rows, :], picked[...], preferred_element_type=jnp.float32)
            moved = source[rows, :].astype(jnp.float32) + mixed_ref[1, rows, :].astype(jnp.float32)
            target[rows, :] = ((moved - 0.5 * drawdown) * (1.0 / 1.5)).astype(jnp.bfloat16)


def proximal_steps(columns, mixed, coefficients):
    _, rows, width = mixed.shape
    return pl.pallas_call(
        steps_kernel,
        out_shape=jax.ShapeDtypeStruct((rows, width), jnp.bfloat16),
        in_specs=[
            pl.BlockSpec(memory_space=pltpu.SMEM),
            pl.BlockSpec(memory_space=pltpu.VMEM),
            pl.BlockSpec(memory_space=pltpu.VMEM),
        ],
        out_specs=pl.BlockSpec(memory_space=pltpu.VMEM),
        scratch_shapes=[
            pltpu.VMEM((2, rows, width), jnp.bfloat16),
            pltpu.VMEM((NB * BLK, width), jnp.bfloat16),
        ],
        compiler_params=pltpu.CompilerParams(vmem_limit_bytes=40 << 20),
    )(columns, mixed, coefficients)


def slot_roles(slot_well, well_owner, sector_count, tile_count):
    wells = well_owner.shape[0]
    self_index = lax.axis_index("sector") * tile_count + lax.axis_index("tile")
    shared = slot_well >= 0
    owner = jnp.sum(
        jnp.where(slot_well[:, None] == jnp.arange(wells)[None, :], well_owner[None, :], 0), axis=1
    )
    home = shared & (owner == self_index)
    away = shared & (owner != self_index)
    bound = (owner[:, None] // tile_count == jnp.arange(sector_count)[None, :]) & away[:, None]
    slots = slot_well.shape[0]
    earlier = jnp.arange(slots)[None, :] < jnp.arange(slots)[:, None]
    before = jnp.dot(
        earlier.astype(jnp.bfloat16), bound.astype(jnp.bfloat16), preferred_element_type=jnp.float32
    )
    position = jnp.sum(jnp.where(bound, before, 0.0), axis=1).astype(jnp.int32)
    place = jnp.where(away, owner // tile_count * CAP + position, -1)
    return shared, home, place


def shards(rates, target, prior_consensus, duals, response, block_cols, slot_well, well_owner):
    slot_count, periods = rates.shape
    sector_count = lax.axis_size("sector")
    tile_count = lax.axis_size("tile")
    buffer_rows = sector_count * CAP
    pulled = (0.5 * target.astype(jnp.float32) + 0.5 * (prior_consensus - duals)).astype(jnp.bfloat16)
    mixed = lax.all_to_all(
        jnp.stack([rates, pulled]), "tile", split_axis=2, concat_axis=1, tiled=True
    )
    coefficients = lax.all_gather(response, "tile", axis=0, tiled=True)
    columns = lax.all_gather(block_cols.reshape(-1), "tile", axis=0, tiled=True)

    shared, home, place = slot_roles(slot_well, well_owner, sector_count, tile_count)
    placing = jnp.arange(buffer_rows)[:, None] == place[None, :]
    send_wells = jnp.max(jnp.where(placing, slot_well[None, :], -1), axis=1)
    got_wells = lax.all_to_all(
        send_wells.reshape(sector_count, CAP), "sector", split_axis=0, concat_axis=0, tiled=True
    ).reshape(buffer_rows)
    matching = (got_wells[:, None] == slot_well[None, :]) & home[None, :]
    weight = 2.0 + jnp.sum(matching.astype(jnp.float32), axis=0)
    placing = placing.astype(jnp.bfloat16)
    matching = matching.astype(jnp.bfloat16)

    last = proximal_steps(columns, mixed, coefficients)
    new_rates = lax.all_to_all(last, "tile", split_axis=0, concat_axis=1, tiled=True)
    rates_wide = new_rates.astype(jnp.float32)
    offered = (rates_wide + duals).astype(jnp.bfloat16)
    send_values = jnp.dot(placing, offered, preferred_element_type=jnp.float32).astype(jnp.bfloat16)
    received = lax.all_to_all(
        send_values.reshape(sector_count, CAP, periods), "sector", split_axis=0, concat_axis=0, tiled=True
    ).reshape(buffer_rows, periods)
    added = lax.dot_general(
        matching, received, (((0,), (0,)), ((), ())), preferred_element_type=jnp.float32
    )
    mean = (2.0 * offered.astype(jnp.float32) + added) / weight[:, None]
    answers = jnp.dot(matching, mean.astype(jnp.bfloat16), preferred_element_type=jnp.float32)
    returned = lax.all_to_all(
        answers.astype(jnp.bfloat16).reshape(sector_count, CAP, periods),
        "sector", split_axis=0, concat_axis=0, tiled=True,
    ).reshape(buffer_rows, periods)
    from_peer = lax.dot_general(
        placing, returned, (((0,), (0,)), ((), ())), preferred_element_type=jnp.float32
    )
    slot_mean = jnp.where(home[:, None], mean, from_peer)
    consensus = jnp.where(shared[:, None], slot_mean, rates_wide)
    new_duals = jnp.where(shared[:, None], duals + rates_wide - consensus, duals)
    return (new_rates, new_duals, consensus)


def solution(mesh):
    both = P(("sector", "tile"), None)
    return jax.shard_map(
        shards,
        mesh=mesh,
        in_specs=(both, both, both, both, both, both, P(("sector", "tile")), P()),
        out_specs=(both, both, both),
        check_vma=False,
    )
```

```python
import functools

import jax
import jax.numpy as jnp
from jax import lax
from jax.experimental import pallas as pl
from jax.experimental.pallas import tpu as pltpu
from jax.sharding import PartitionSpec as P

NB = 4
INNER = 3
CAP = 4
BLK = 128
TILES = 4
SLAB = CAP * TILES
MESH = pl.DeviceIdType.MESH


def round_kernel(
    sectors,
    rates, target, prior, duals, response, cols, roles, role_cols,
    new_rates, new_duals, consensus,
    start, pull, pull_out, coef, state, last, got_rates, drawn, dense,
    cols_all, target_v, prior_v, duals_v, placing, matching,
    wells_out, wells_in, offered, values_out, values_in, answers_out, answers_in, mean, duals_o, cons_o,
    local_sem, tile_send, tile_recv, sector_send, sector_recv, out_sem,
):
    slots, periods = rates.shape
    width = periods // TILES
    own = lax.axis_index("tile")
    sector = lax.axis_index("sector")
    peer = [own, own + 1 - 2 * (own % 2), (own + 2) % TILES, TILES - 1 - own]

    def slot_rows(tile):
        return pl.ds(pl.multiple_of(tile * slots, slots), slots)

    def share(tile):
        return pl.ds(pl.multiple_of(tile * width, width), width)

    def to_tile(phase, k, source, dest, via=None):
        return pltpu.make_async_remote_copy(
            src_ref=source, dst_ref=dest,
            send_sem=tile_send.at[phase, k], recv_sem=tile_recv.at[phase, k],
            device_id={"tile": peer[k if via is None else via]}, device_id_type=MESH,
        )

    def to_sector(phase, j, source, dest):
        return pltpu.make_async_remote_copy(
            src_ref=source, dst_ref=dest,
            send_sem=sector_send.at[phase, j], recv_sem=sector_recv.at[phase, j],
            device_id={"sector": lax.rem(sector + j, sectors)}, device_id_type=MESH,
        )

    def slab(index):
        return pl.ds(pl.multiple_of(index * SLAB, SLAB), SLAB)

    barrier = pltpu.get_barrier_semaphore()
    for k in range(1, TILES):
        pl.semaphore_signal(barrier, inc=1, device_id={"tile": peer[k]}, device_id_type=MESH)

    @pl.loop(1, sectors)
    def _(j):
        pl.semaphore_signal(
            barrier, inc=1, device_id={"sector": lax.rem(sector + j, sectors)}, device_id_type=MESH
        )

    loads = [
        pltpu.make_async_copy(a, b, local_sem.at[i])
        for i, (a, b) in enumerate([
            (target, target_v), (prior, prior_v), (duals, duals_v),
            (rates.at[:, share(own)], start.at[slot_rows(own), :]),
            (response, coef.at[slot_rows(own), :]),
        ])
    ]
    for copy in loads:
        copy.start()
    col_count = cols.shape[0]

    def col_rows_of(tile):
        return pl.ds(pl.multiple_of(tile * col_count, col_count), col_count)

    col_rows = col_rows_of(own)
    cols_all[col_rows, :] = cols[...]
    pl.semaphore_wait(barrier, TILES - 1 + sectors - 1)

    sends = []

    def send(phase, k, source, dest, via=None):
        copy = to_tile(phase, k, source, dest, via)
        copy.start()
        sends.append(copy)

    for k in (2, 3, 1):
        send(0, k, cols, cols_all.at[col_rows, :])
    send(1, 2, response, coef.at[slot_rows(own), :])
    for k in (2, 3):
        send(2, k, rates.at[:, share(peer[k])], start.at[slot_rows(own), :])
    send(1, 1, response, coef.at[slot_rows(own), :])
    send(2, 1, rates.at[:, share(peer[1])], start.at[slot_rows(own), :])

    for copy in loads[:3]:
        copy.wait()

    def pull_of(k):
        at = share(peer[k])
        value = 0.5 * target_v[:, at].astype(jnp.float32) + 0.5 * (prior_v[:, at] - duals_v[:, at])
        return value.astype(jnp.bfloat16)

    for k in (2, 3, 1):
        pull_out[k] = pull_of(k)
        send(3, k, pull_out.at[k], pull.at[slot_rows(own), :])
    pull[slot_rows(own), :] = pull_of(0)

    place_row, well_row, home_row = roles[0:1, :], roles[1:2, :], roles[2:3, :] > 0
    row = lax.broadcasted_iota(jnp.int32, (sectors * SLAB, 1), 0)
    chunk = (row % SLAB) // CAP
    placed = place_row == (row // SLAB) * CAP + row % CAP
    wells = jnp.max(jnp.where(placed, well_row, -1), axis=1, keepdims=True)
    wells_out[...] = jnp.broadcast_to(wells, wells_out.shape)
    for q in range(TILES):
        placing[q] = jnp.where(placed & (chunk == q), 1.0, 0.0).astype(jnp.bfloat16)
    wells_in[slab(sector), :] = jnp.full((SLAB, 128), -1, jnp.int32)
    values_in[slab(sector), :] = jnp.zeros((SLAB, width), jnp.bfloat16)
    answers_in[slab(sector), :] = jnp.zeros((SLAB, width), jnp.bfloat16)

    def exchange(phase, source, dest):
        @pl.loop(1, sectors)
        def _(j):
            to_sector(
                phase, j, source.at[slab(lax.rem(sector + j, sectors)), :], dest.at[slab(sector), :]
            ).start()

    def arrived(phase, source, dest):
        @pl.loop(1, sectors)
        def _(j):
            to_sector(
                phase, j, source.at[slab(lax.rem(sector + j, sectors)), :],
                dest.at[slab(lax.rem(sector + sectors - j, sectors)), :],
            ).wait()

    exchange(0, wells_out, wells_in)

    def recv(phase, k, ref):
        to_tile(phase, k, ref, ref).wait_recv()

    per_tile = slots // BLK

    def expand(tile):
        names = cols_all[col_rows_of(tile), :]
        for inner in range(per_tile):
            rows = pl.ds(pl.multiple_of(tile * slots + inner * BLK, BLK), BLK)
            blocks = [coef[rows, n * BLK : (n + 1) * BLK].astype(jnp.float32) for n in range(NB)]
            for c in range(per_tile * TILES):
                value = jnp.zeros((BLK, BLK), jnp.float32)
                for n in range(NB):
                    name = names[inner * NB + n : inner * NB + n + 1, :]
                    value = jnp.where(name == c, blocks[n], value)
                dense[rows, c * BLK : (c + 1) * BLK] = value.astype(jnp.bfloat16)

    recv(1, 2, coef.at[slot_rows(peer[2]), :])
    send(1, 3, coef.at[slot_rows(peer[2]), :], coef.at[slot_rows(peer[2]), :], 1)
    arrived(0, wells_out, wells_in)
    match = (wells_in[:, 0:1] == well_row) & home_row
    for q in range(TILES):
        matching[q] = jnp.where(match & (chunk == q), 1.0, 0.0).astype(jnp.bfloat16)
    heard = lax.dot_general(
        matching[0], jnp.ones((sectors * SLAB, 128), jnp.bfloat16),
        (((0,), (0,)), ((), ())), preferred_element_type=jnp.float32,
    )
    scale = 1.0 / (2.0 + heard[:, 0:1])

    for copy in loads[3:]:
        copy.wait()
    for k in (1, 2, 3):
        recv(0, k, cols_all.at[col_rows_of(peer[k]), :])
    expand(own)
    recv(1, 1, coef.at[slot_rows(peer[1]), :])
    expand(peer[1])
    expand(peer[2])
    recv(1, 3, coef.at[slot_rows(peer[3]), :])
    expand(peer[3])
    for k in (1, 2, 3):
        recv(2, k, start.at[slot_rows(peer[k]), :])

    part = 256

    def drawdown(at, source):
        rows = pl.ds(pl.multiple_of(at, part), part)
        return rows, jnp.dot(dense[rows, :], source[...], preferred_element_type=jnp.float32)

    def stepped(rows, source, drawn_rows):
        moved = source[rows, :].astype(jnp.float32) + pull[rows, :].astype(jnp.float32)
        return ((moved - 0.5 * drawn_rows) * (1.0 / 1.5)).astype(jnp.bfloat16)

    @pl.loop(0, slots * TILES // part)
    def _(block):
        rows, value = drawdown(block * part, start)
        drawn[rows, :] = value

    for k in (1, 2, 3):
        recv(3, k, pull.at[slot_rows(peer[k]), :])

    @pl.loop(0, per_tile * TILES)
    def _(block):
        rows = pl.ds(pl.multiple_of(block * BLK, BLK), BLK)
        state[0, rows, :] = stepped(rows, start, drawn[rows, :])

    for step in range(1, INNER - 1):
        source = state.at[(step + 1) % 2]
        dest = state.at[step % 2]

        @pl.loop(0, slots * TILES // part)
        def _(block):
            rows, value = drawdown(block * part, source)
            dest[rows, :] = stepped(rows, source, value)

    source = state.at[INNER % 2]
    for k in (2, 3, 1, 0):
        for inner in range(slots // part):
            rows, value = drawdown(peer[k] * slots + inner * part, source)
            result = stepped(rows, source, value)
            if k == 0:
                got_rates[own, inner * part : (inner + 1) * part, :] = result
            else:
                last[k, inner * part : (inner + 1) * part, :] = result
        if k > 0:
            send(4, k, last.at[k], got_rates.at[own])

    outs = []

    def put(i, source, dest):
        copy = pltpu.make_async_copy(source, dest, out_sem.at[i])
        copy.start()
        outs.append(copy)

    total = jnp.zeros((sectors * SLAB, width), jnp.float32)
    for k in range(TILES):
        q = peer[k]
        if k > 0:
            recv(4, k, got_rates.at[q])
        put(k, got_rates.at[q], new_rates.at[:, share(q)])
        offer = (got_rates[q].astype(jnp.float32) + duals_v[:, share(q)]).astype(jnp.bfloat16)
        offered[k] = offer
        total += jnp.dot(placing[q], offer, preferred_element_type=jnp.float32)
    values_out[...] = total.astype(jnp.bfloat16)
    exchange(1, values_out, values_in)
    arrived(1, values_out, values_in)
    total = jnp.zeros((sectors * SLAB, width), jnp.float32)
    for k in range(TILES):
        q = peer[k]
        added = lax.dot_general(
            matching[q], values_in[...], (((0,), (0,)), ((), ())), preferred_element_type=jnp.float32
        )
        value = (2.0 * offered[k].astype(jnp.float32) + added) * scale
        mean[k] = value
        total += jnp.dot(matching[q], value.astype(jnp.bfloat16), preferred_element_type=jnp.float32)
    answers_out[...] = total.astype(jnp.bfloat16)
    exchange(2, answers_out, answers_in)
    home, shared = role_cols[:, 0:1] > 0, role_cols[:, 1:2] > 0
    arrived(2, answers_out, answers_in)
    for k in range(TILES):
        q = peer[k]
        from_peer = lax.dot_general(
            placing[q], answers_in[...], (((0,), (0,)), ((), ())), preferred_element_type=jnp.float32
        )
        wide = got_rates[q].astype(jnp.float32)
        agreed = jnp.where(home, mean[k], jnp.where(shared, from_peer, wide))
        cons_o[k] = agreed
        put(4 + k, cons_o.at[k], consensus.at[:, share(q)])
        kept = duals_v[:, share(q)]
        duals_o[k] = jnp.where(shared, kept + wide - agreed, kept)
        put(8 + k, duals_o.at[k], new_duals.at[:, share(q)])
    for copy in outs:
        copy.wait()
    for copy in sends:
        copy.wait_send()


def slot_roles(slot_well, well_owner, sector_count, tile_count):
    wells = well_owner.shape[0]
    self_index = lax.axis_index("sector") * tile_count + lax.axis_index("tile")
    shared = slot_well >= 0
    owner = jnp.sum(
        jnp.where(slot_well[:, None] == jnp.arange(wells)[None, :], well_owner[None, :], 0), axis=1
    )
    home = shared & (owner == self_index)
    away = shared & (owner != self_index)
    bound = (owner[:, None] // tile_count == jnp.arange(sector_count)[None, :]) & away[:, None]
    slots = slot_well.shape[0]
    earlier = jnp.arange(slots)[None, :] < jnp.arange(slots)[:, None]
    before = jnp.dot(
        earlier.astype(jnp.bfloat16), bound.astype(jnp.bfloat16), preferred_element_type=jnp.float32
    )
    position = jnp.sum(jnp.where(bound, before, 0.0), axis=1).astype(jnp.int32)
    place = jnp.where(away, owner // tile_count * CAP + position, -1)
    return shared, home, place


def shards(rates, target, prior_consensus, duals, response, block_cols, slot_well, well_owner):
    slots, periods = rates.shape
    sectors = lax.axis_size("sector")
    width = periods // TILES
    rows = TILES * slots
    slabs = sectors * SLAB
    shared, home, place = slot_roles(slot_well, well_owner, sectors, TILES)
    shared, home = shared.astype(jnp.int32), home.astype(jnp.int32)
    empty = jnp.zeros_like(place)
    roles = jnp.stack([place, slot_well, home] + [empty] * 5)
    role_cols = jnp.stack([home, shared], axis=1)
    cols = jnp.broadcast_to(block_cols.reshape(-1, 1), (block_cols.size, 128))
    bf16, f32, i32 = jnp.bfloat16, jnp.float32, jnp.int32
    whole = pl.BlockSpec(memory_space=pltpu.VMEM)
    far = pl.BlockSpec(memory_space=pl.ANY)
    dma = pltpu.SemaphoreType.DMA
    return pl.pallas_call(
        functools.partial(round_kernel, sectors),
        out_shape=(
            jax.ShapeDtypeStruct((slots, periods), bf16),
            jax.ShapeDtypeStruct((slots, periods), f32),
            jax.ShapeDtypeStruct((slots, periods), f32),
        ),
        in_specs=[far] * 5 + [whole] * 3,
        out_specs=(far, far, far),
        scratch_shapes=[
            pltpu.VMEM((rows, width), bf16),
            pltpu.VMEM((rows, width), bf16),
            pltpu.VMEM((TILES, slots, width), bf16),
            pltpu.VMEM((rows, NB * BLK), bf16),
            pltpu.VMEM((2, rows, width), bf16),
            pltpu.VMEM((TILES, slots, width), bf16),
            pltpu.VMEM((TILES, slots, width), bf16),
            pltpu.VMEM((rows, width), f32),
            pltpu.VMEM((rows, rows), bf16),
            pltpu.VMEM((TILES * block_cols.size, 128), i32),
            pltpu.VMEM((slots, periods), bf16),
            pltpu.VMEM((slots, periods), f32),
            pltpu.VMEM((slots, periods), f32),
            pltpu.VMEM((TILES, slabs, slots), bf16),
            pltpu.VMEM((TILES, slabs, slots), bf16),
            pltpu.VMEM((slabs, 128), i32),
            pltpu.VMEM((slabs, 128), i32),
            pltpu.VMEM((TILES, slots, width), bf16),
            pltpu.VMEM((slabs, width), bf16),
            pltpu.VMEM((slabs, width), bf16),
            pltpu.VMEM((slabs, width), bf16),
            pltpu.VMEM((slabs, width), bf16),
            pltpu.VMEM((TILES, slots, width), f32),
            pltpu.VMEM((TILES, slots, width), f32),
            pltpu.VMEM((TILES, slots, width), f32),
            dma((5,)),
            dma((5, TILES)),
            dma((5, TILES)),
            dma((3, sectors)),
            dma((3, sectors)),
            dma((12,)),
        ],
        compiler_params=pltpu.CompilerParams(
            collective_id=0, has_side_effects=True, vmem_limit_bytes=56 << 20
        ),
    )(rates, target, prior_consensus, duals, response, cols, roles, role_cols)


def solution(mesh):
    both = P(("sector", "tile"), None)
    return jax.shard_map(
        shards,
        mesh=mesh,
        in_specs=(both, both, both, both, both, both, P(("sector", "tile")), P()),
        out_specs=(both, both, both),
        check_vma=False,
    )
```

```python
import functools

import jax
import jax.numpy as jnp
from jax import lax
from jax.experimental import pallas as pl
from jax.experimental.pallas import tpu as pltpu
from jax.sharding import PartitionSpec as P

NB = 4
INNER = 3
CAP = 4
BLK = 128
TILES = 4
SLAB = CAP * TILES
MESH = pl.DeviceIdType.MESH


def round_kernel(
    sectors,
    rates, target, prior, duals, response, cols, slot_well, well_owner,
    rates_o, placing_o, matching_o, values_o, answers_o, roles_o,
    start, pull, pull_out, coef, state, last, got_rates, drawn, dense,
    cols_all, target_v, prior_v, duals_v, placing, matching,
    wells_out, wells_in, offered, values_out, values_in, answers_out, answers_in, roles_v,
    local_sem, tile_send, tile_recv, sector_send, sector_recv, out_sem,
):
    slots, periods = rates.shape
    width = periods // TILES
    own = lax.axis_index("tile")
    sector = lax.axis_index("sector")
    peer = [own, own + 1 - 2 * (own % 2), (own + 2) % TILES, TILES - 1 - own]

    def slot_rows(tile):
        return pl.ds(pl.multiple_of(tile * slots, slots), slots)

    def share(tile):
        return pl.ds(pl.multiple_of(tile * width, width), width)

    def to_tile(phase, k, source, dest, via=None):
        return pltpu.make_async_remote_copy(
            src_ref=source, dst_ref=dest,
            send_sem=tile_send.at[phase, k], recv_sem=tile_recv.at[phase, k],
            device_id={"tile": peer[k if via is None else via]}, device_id_type=MESH,
        )

    def to_sector(phase, j, source, dest):
        return pltpu.make_async_remote_copy(
            src_ref=source, dst_ref=dest,
            send_sem=sector_send.at[phase, j], recv_sem=sector_recv.at[phase, j],
            device_id={"sector": lax.rem(sector + j, sectors)}, device_id_type=MESH,
        )

    def slab(index):
        return pl.ds(pl.multiple_of(index * SLAB, SLAB), SLAB)

    barrier = pltpu.get_barrier_semaphore()
    for k in range(1, TILES):
        pl.semaphore_signal(barrier, inc=1, device_id={"tile": peer[k]}, device_id_type=MESH)

    @pl.loop(1, sectors)
    def _(j):
        pl.semaphore_signal(
            barrier, inc=1, device_id={"sector": lax.rem(sector + j, sectors)}, device_id_type=MESH
        )

    loads = [
        pltpu.make_async_copy(a, b, local_sem.at[i])
        for i, (a, b) in enumerate([
            (target, target_v), (prior, prior_v), (duals, duals_v),
            (rates.at[:, share(own)], start.at[slot_rows(own), :]),
            (response, coef.at[slot_rows(own), :]),
        ])
    ]
    for copy in loads:
        copy.start()
    col_count = cols.shape[0]

    def col_rows_of(tile):
        return pl.ds(pl.multiple_of(tile * col_count, col_count), col_count)

    col_rows = col_rows_of(own)
    cols_all[col_rows, :] = cols[...]
    pl.semaphore_wait(barrier, TILES - 1 + sectors - 1)

    sends = []

    def send(phase, k, source, dest, via=None):
        copy = to_tile(phase, k, source, dest, via)
        copy.start()
        sends.append(copy)

    for k in (2, 3, 1):
        send(0, k, cols, cols_all.at[col_rows, :])
    send(1, 2, response, coef.at[slot_rows(own), :])
    for k in (2, 3):
        send(2, k, rates.at[:, share(peer[k])], start.at[slot_rows(own), :])
    send(1, 1, response, coef.at[slot_rows(own), :])
    send(2, 1, rates.at[:, share(peer[1])], start.at[slot_rows(own), :])

    for copy in loads[:3]:
        copy.wait()

    def pull_of(k):
        at = share(peer[k])
        value = 0.5 * target_v[:, at].astype(jnp.float32) + 0.5 * (prior_v[:, at] - duals_v[:, at])
        return value.astype(jnp.bfloat16)

    for k in (2, 3, 1):
        pull_out[k] = pull_of(k)
        send(3, k, pull_out.at[k], pull.at[slot_rows(own), :])
    pull[slot_rows(own), :] = pull_of(0)

    well_row = slot_well[...]
    group = 512

    def looked_up(i, found):
        at = pl.multiple_of(i * group, group)
        name = lax.broadcasted_iota(jnp.int32, (group, 1), 0) + at
        hit = jnp.where(name == well_row, 1.0, 0.0).astype(jnp.bfloat16)
        owners = jnp.broadcast_to(well_owner[:, pl.ds(at, group)].astype(jnp.float32), (8, group))
        return found + jnp.dot(
            owners.astype(jnp.bfloat16), hit, preferred_element_type=jnp.float32
        )

    owner = lax.fori_loop(
        0, well_owner.shape[1] // group, looked_up, jnp.zeros((8, slots), jnp.float32)
    )[0:1, :].astype(jnp.int32)
    shared_row = well_row >= 0
    home_row = shared_row & (owner == sector * TILES + own)
    away_row = shared_row & (owner != sector * TILES + own)
    facing = owner // TILES
    bound = jnp.where(
        (lax.broadcasted_iota(jnp.int32, (sectors, 1), 0) == facing) & away_row, 1.0, 0.0
    )
    earlier = jnp.where(
        lax.broadcasted_iota(jnp.int32, (slots, 1), 0) < lax.broadcasted_iota(jnp.int32, (1, slots), 1),
        1.0, 0.0,
    )
    before = jnp.dot(
        bound.astype(jnp.bfloat16), earlier.astype(jnp.bfloat16), preferred_element_type=jnp.float32
    )
    position = jnp.sum(bound * before, axis=0, keepdims=True).astype(jnp.int32)
    place_row = jnp.where(away_row, facing * CAP + position, -1)
    row = lax.broadcasted_iota(jnp.int32, (sectors * SLAB, 1), 0)
    chunk = (row % SLAB) // CAP
    placed = place_row == (row // SLAB) * CAP + row % CAP
    wells = jnp.max(jnp.where(placed, well_row, -1), axis=1, keepdims=True)
    wells_out[...] = jnp.broadcast_to(wells, wells_out.shape)
    for q in range(TILES):
        placing[q] = jnp.where(placed & (chunk == q), 1.0, 0.0).astype(jnp.bfloat16)
    wells_in[slab(sector), :] = jnp.full((SLAB, 128), -1, jnp.int32)
    values_in[slab(sector), :] = jnp.zeros((SLAB, width), jnp.bfloat16)
    answers_in[slab(sector), :] = jnp.zeros((SLAB, width), jnp.bfloat16)

    def exchange(phase, source, dest):
        @pl.loop(1, sectors)
        def _(j):
            to_sector(
                phase, j, source.at[slab(lax.rem(sector + j, sectors)), :], dest.at[slab(sector), :]
            ).start()

    def arrived(phase, source, dest):
        @pl.loop(1, sectors)
        def _(j):
            to_sector(
                phase, j, source.at[slab(lax.rem(sector + j, sectors)), :],
                dest.at[slab(lax.rem(sector + sectors - j, sectors)), :],
            ).wait()

    exchange(0, wells_out, wells_in)

    def recv(phase, k, ref):
        to_tile(phase, k, ref, ref).wait_recv()

    per_tile = slots // BLK

    def expand(tile):
        names = cols_all[col_rows_of(tile), :]
        for inner in range(per_tile):
            rows = pl.ds(pl.multiple_of(tile * slots + inner * BLK, BLK), BLK)
            blocks = [coef[rows, n * BLK : (n + 1) * BLK].astype(jnp.float32) for n in range(NB)]
            for c in range(per_tile * TILES):
                value = jnp.zeros((BLK, BLK), jnp.float32)
                for n in range(NB):
                    name = names[inner * NB + n : inner * NB + n + 1, :]
                    value = jnp.where(name == c, blocks[n], value)
                dense[rows, c * BLK : (c + 1) * BLK] = value.astype(jnp.bfloat16)

    recv(1, 2, coef.at[slot_rows(peer[2]), :])
    send(1, 3, coef.at[slot_rows(peer[2]), :], coef.at[slot_rows(peer[2]), :], 1)
    arrived(0, wells_out, wells_in)
    match = (wells_in[:, 0:1] == well_row) & home_row
    for q in range(TILES):
        matching[q] = jnp.where(match & (chunk == q), 1.0, 0.0).astype(jnp.bfloat16)
    heard = lax.dot_general(
        matching[0], jnp.ones((sectors * SLAB, 128), jnp.bfloat16),
        (((0,), (0,)), ((), ())), preferred_element_type=jnp.float32,
    )
    scale = 1.0 / (2.0 + heard)
    roles_v[0] = scale
    kind = jnp.where(home_row, 2.0, jnp.where(shared_row, 1.0, 0.0))
    roles_v[1] = jnp.broadcast_to(kind, (128, slots)).T
    scale = scale[:, 0:1]
    outs = []

    def put(i, source, dest):
        copy = pltpu.make_async_copy(source, dest, out_sem.at[i])
        copy.start()
        outs.append(copy)

    put(4, placing, placing_o)
    put(5, matching, matching_o)
    put(6, roles_v, roles_o)

    for copy in loads[3:]:
        copy.wait()
    for k in (1, 2, 3):
        recv(0, k, cols_all.at[col_rows_of(peer[k]), :])
    expand(own)
    recv(1, 1, coef.at[slot_rows(peer[1]), :])
    expand(peer[1])
    expand(peer[2])
    recv(1, 3, coef.at[slot_rows(peer[3]), :])
    expand(peer[3])
    for k in (1, 2, 3):
        recv(2, k, start.at[slot_rows(peer[k]), :])

    part = 256

    def drawdown(at, source):
        rows = pl.ds(pl.multiple_of(at, part), part)
        return rows, jnp.dot(dense[rows, :], source[...], preferred_element_type=jnp.float32)

    def stepped(rows, source, drawn_rows):
        moved = source[rows, :].astype(jnp.float32) + pull[rows, :].astype(jnp.float32)
        return ((moved - 0.5 * drawn_rows) * (1.0 / 1.5)).astype(jnp.bfloat16)

    @pl.loop(0, slots * TILES // part)
    def _(block):
        rows, value = drawdown(block * part, start)
        drawn[rows, :] = value

    for k in (1, 2, 3):
        recv(3, k, pull.at[slot_rows(peer[k]), :])

    @pl.loop(0, per_tile * TILES)
    def _(block):
        rows = pl.ds(pl.multiple_of(block * BLK, BLK), BLK)
        state[0, rows, :] = stepped(rows, start, drawn[rows, :])

    for step in range(1, INNER - 1):
        source = state.at[(step + 1) % 2]
        dest = state.at[step % 2]

        @pl.loop(0, slots * TILES // part)
        def _(block):
            rows, value = drawdown(block * part, source)
            dest[rows, :] = stepped(rows, source, value)

    source = state.at[INNER % 2]
    for k in (2, 3, 1, 0):
        for inner in range(slots // part):
            rows, value = drawdown(peer[k] * slots + inner * part, source)
            result = stepped(rows, source, value)
            if k == 0:
                got_rates[own, inner * part : (inner + 1) * part, :] = result
            else:
                last[k, inner * part : (inner + 1) * part, :] = result
        if k > 0:
            send(4, k, last.at[k], got_rates.at[own])

    total = jnp.zeros((sectors * SLAB, width), jnp.float32)
    for k in range(TILES):
        q = peer[k]
        if k > 0:
            recv(4, k, got_rates.at[q])
        put(k, got_rates.at[q], rates_o.at[q])
        offer = (got_rates[q].astype(jnp.float32) + duals_v[:, share(q)]).astype(jnp.bfloat16)
        offered[k] = offer
        total += jnp.dot(placing[q], offer, preferred_element_type=jnp.float32)
    values_out[...] = total.astype(jnp.bfloat16)
    exchange(1, values_out, values_in)
    arrived(1, values_out, values_in)
    put(7, values_in, values_o)
    total = jnp.zeros((sectors * SLAB, width), jnp.float32)
    for k in range(TILES):
        q = peer[k]
        added = lax.dot_general(
            matching[q], values_in[...], (((0,), (0,)), ((), ())), preferred_element_type=jnp.float32
        )
        value = (2.0 * offered[k].astype(jnp.float32) + added) * scale
        total += jnp.dot(matching[q], value.astype(jnp.bfloat16), preferred_element_type=jnp.float32)
    answers_out[...] = total.astype(jnp.bfloat16)
    exchange(2, answers_out, answers_in)
    arrived(2, answers_out, answers_in)
    put(8, answers_in, answers_o)
    for copy in outs:
        copy.wait()
    for copy in sends:
        copy.wait_send()


def outputs_kernel(
    rates, duals, placing, matching, values, answers, roles, new_rates, new_duals, consensus
):
    ours = (((0,), (0,)), ((), ()))
    added = lax.dot_general(matching[0], values[...], ours, preferred_element_type=jnp.float32)
    from_peer = lax.dot_general(placing[0], answers[...], ours, preferred_element_type=jnp.float32)
    scale, kind = roles[0, :, 0:1], roles[1, :, 0:1]
    wide, kept = rates[0].astype(jnp.float32), duals[...]
    offer = (wide + kept).astype(jnp.bfloat16).astype(jnp.float32)
    mean = (2.0 * offer + added) * scale
    agreed = jnp.where(kind > 1.5, mean, jnp.where(kind > 0.5, from_peer, wide))
    new_rates[...] = rates[0]
    consensus[...] = agreed
    new_duals[...] = jnp.where(kind > 0.5, kept + wide - agreed, kept)


def shards(rates, target, prior_consensus, duals, response, block_cols, slot_well, well_owner):
    slots, periods = rates.shape
    sectors = lax.axis_size("sector")
    width = periods // TILES
    rows = TILES * slots
    slabs = sectors * SLAB
    cols = jnp.broadcast_to(block_cols.reshape(-1, 1), (block_cols.size, 128))
    bf16, f32, i32 = jnp.bfloat16, jnp.float32, jnp.int32
    whole = pl.BlockSpec(memory_space=pltpu.VMEM)
    far = pl.BlockSpec(memory_space=pl.ANY)
    dma = pltpu.SemaphoreType.DMA
    moved = pl.pallas_call(
        functools.partial(round_kernel, sectors),
        out_shape=(
            jax.ShapeDtypeStruct((TILES, slots, width), bf16),
            jax.ShapeDtypeStruct((TILES, slabs, slots), bf16),
            jax.ShapeDtypeStruct((TILES, slabs, slots), bf16),
            jax.ShapeDtypeStruct((slabs, width), bf16),
            jax.ShapeDtypeStruct((slabs, width), bf16),
            jax.ShapeDtypeStruct((2, slots, 128), f32),
        ),
        in_specs=[far] * 5 + [whole] * 3,
        out_specs=(far,) * 6,
        scratch_shapes=[
            pltpu.VMEM((rows, width), bf16),
            pltpu.VMEM((rows, width), bf16),
            pltpu.VMEM((TILES, slots, width), bf16),
            pltpu.VMEM((rows, NB * BLK), bf16),
            pltpu.VMEM((2, rows, width), bf16),
            pltpu.VMEM((TILES, slots, width), bf16),
            pltpu.VMEM((TILES, slots, width), bf16),
            pltpu.VMEM((rows, width), f32),
            pltpu.VMEM((rows, rows), bf16),
            pltpu.VMEM((TILES * block_cols.size, 128), i32),
            pltpu.VMEM((slots, periods), bf16),
            pltpu.VMEM((slots, periods), f32),
            pltpu.VMEM((slots, periods), f32),
            pltpu.VMEM((TILES, slabs, slots), bf16),
            pltpu.VMEM((TILES, slabs, slots), bf16),
            pltpu.VMEM((slabs, 128), i32),
            pltpu.VMEM((slabs, 128), i32),
            pltpu.VMEM((TILES, slots, width), bf16),
            pltpu.VMEM((slabs, width), bf16),
            pltpu.VMEM((slabs, width), bf16),
            pltpu.VMEM((slabs, width), bf16),
            pltpu.VMEM((slabs, width), bf16),
            pltpu.VMEM((2, slots, 128), f32),
            dma((5,)),
            dma((5, TILES)),
            dma((5, TILES)),
            dma((3, sectors)),
            dma((3, sectors)),
            dma((9,)),
        ],
        compiler_params=pltpu.CompilerParams(
            collective_id=0, has_side_effects=True, vmem_limit_bytes=56 << 20
        ),
    )(rates, target, prior_consensus, duals, response, cols, slot_well.reshape(1, -1), well_owner.reshape(1, -1))
    columns = pl.BlockSpec((slots, width), lambda q: (0, q))
    picks = pl.BlockSpec((1, slabs, slots), lambda q: (q, 0, 0))
    rows_sent = pl.BlockSpec((slabs, width), lambda q: (0, 0))
    return pl.pallas_call(
        outputs_kernel,
        grid=(TILES,),
        out_shape=(
            jax.ShapeDtypeStruct((slots, periods), bf16),
            jax.ShapeDtypeStruct((slots, periods), f32),
            jax.ShapeDtypeStruct((slots, periods), f32),
        ),
        in_specs=[
            pl.BlockSpec((1, slots, width), lambda q: (q, 0, 0)),
            columns, picks, picks, rows_sent, rows_sent,
            pl.BlockSpec((2, slots, 128), lambda q: (0, 0, 0)),
        ],
        out_specs=(columns, columns, columns),
        compiler_params=pltpu.CompilerParams(vmem_limit_bytes=40 << 20),
    )(moved[0], duals, *moved[1:])


def solution(mesh):
    both = P(("sector", "tile"), None)
    return jax.shard_map(
        shards,
        mesh=mesh,
        in_specs=(both, both, both, both, both, both, P(("sector", "tile")), P()),
        out_specs=(both, both, both),
        check_vma=False,
    )
```

```python
import functools

import jax
import jax.numpy as jnp
from jax import lax
from jax.experimental import pallas as pl
from jax.experimental.pallas import tpu as pltpu
from jax.sharding import PartitionSpec as P

NB = 4
INNER = 3
CAP = 4
BLK = 128
TILES = 4
SLAB = CAP * TILES
MESH = pl.DeviceIdType.MESH


def round_kernel(
    sectors,
    rates, target, prior, duals, response, cols, slot_well, well_owner,
    rates_o, placing_o, matching_o, values_o, answers_o, roles_o,
    start, pull, pull_out, coef, state, last, got_rates, drawn, dense,
    cols_all, target_v, prior_v, duals_v, placing, matching,
    wells_out, wells_in, offered, values_out, values_in, answers_out, answers_in, roles_v,
    local_sem, tile_send, tile_recv, sector_send, sector_recv, out_sem,
):
    slots, periods = rates.shape
    width = periods // TILES
    own = lax.axis_index("tile")
    sector = lax.axis_index("sector")
    peer = [own, own + 1 - 2 * (own % 2), (own + 2) % TILES, TILES - 1 - own]

    def slot_rows(tile):
        return pl.ds(pl.multiple_of(tile * slots, slots), slots)

    def share(tile):
        return pl.ds(pl.multiple_of(tile * width, width), width)

    def to_tile(phase, k, source, dest, via=None):
        return pltpu.make_async_remote_copy(
            src_ref=source, dst_ref=dest,
            send_sem=tile_send.at[phase, k], recv_sem=tile_recv.at[phase, k],
            device_id={"tile": peer[k if via is None else via]}, device_id_type=MESH,
        )

    def to_sector(phase, j, source, dest):
        return pltpu.make_async_remote_copy(
            src_ref=source, dst_ref=dest,
            send_sem=sector_send.at[phase, j], recv_sem=sector_recv.at[phase, j],
            device_id={"sector": lax.rem(sector + j, sectors)}, device_id_type=MESH,
        )

    def slab(index):
        return pl.ds(pl.multiple_of(index * SLAB, SLAB), SLAB)

    barrier = pltpu.get_barrier_semaphore()
    for k in range(1, TILES):
        pl.semaphore_signal(barrier, inc=1, device_id={"tile": peer[k]}, device_id_type=MESH)

    @pl.loop(1, sectors)
    def _(j):
        pl.semaphore_signal(
            barrier, inc=1, device_id={"sector": lax.rem(sector + j, sectors)}, device_id_type=MESH
        )

    loads = [
        pltpu.make_async_copy(a, b, local_sem.at[i])
        for i, (a, b) in enumerate([
            (target, target_v), (prior, prior_v), (duals, duals_v),
            (rates.at[:, share(own)], start.at[slot_rows(own), :]),
            (response, coef.at[slot_rows(own), :]),
        ])
    ]
    for copy in loads:
        copy.start()
    col_count = cols.shape[0]

    def col_rows_of(tile):
        return pl.ds(pl.multiple_of(tile * col_count, col_count), col_count)

    col_rows = col_rows_of(own)
    cols_all[col_rows, :] = cols[...]
    pl.semaphore_wait(barrier, TILES - 1 + sectors - 1)

    sends = []

    def send(phase, k, source, dest, via=None):
        copy = to_tile(phase, k, source, dest, via)
        copy.start()
        sends.append(copy)

    for k in (2, 3, 1):
        send(0, k, cols, cols_all.at[col_rows, :])
    send(1, 2, response, coef.at[slot_rows(own), :])
    for k in (2, 3):
        send(2, k, rates.at[:, share(peer[k])], start.at[slot_rows(own), :])
    send(1, 1, response, coef.at[slot_rows(own), :])
    send(2, 1, rates.at[:, share(peer[1])], start.at[slot_rows(own), :])

    for copy in loads[:3]:
        copy.wait()

    def pull_of(k):
        at = share(peer[k])
        value = 0.5 * target_v[:, at].astype(jnp.float32) + 0.5 * (prior_v[:, at] - duals_v[:, at])
        return value.astype(jnp.bfloat16)

    for k in (2, 3, 1):
        pull_out[k] = pull_of(k)
        send(3, k, pull_out.at[k], pull.at[slot_rows(own), :])
    pull[slot_rows(own), :] = pull_of(0)

    well_row = slot_well[...]
    group = 512

    def looked_up(i, found):
        at = pl.multiple_of(i * group, group)
        name = lax.broadcasted_iota(jnp.int32, (group, 1), 0) + at
        hit = jnp.where(name == well_row, 1.0, 0.0).astype(jnp.bfloat16)
        owners = jnp.broadcast_to(well_owner[:, pl.ds(at, group)].astype(jnp.float32), (8, group))
        return found + jnp.dot(
            owners.astype(jnp.bfloat16), hit, preferred_element_type=jnp.float32
        )

    owner = lax.fori_loop(
        0, well_owner.shape[1] // group, looked_up, jnp.zeros((8, slots), jnp.float32)
    )[0:1, :].astype(jnp.int32)
    shared_row = well_row >= 0
    home_row = shared_row & (owner == sector * TILES + own)
    away_row = shared_row & (owner != sector * TILES + own)
    facing = owner // TILES
    bound = jnp.where(
        (lax.broadcasted_iota(jnp.int32, (sectors, 1), 0) == facing) & away_row, 1.0, 0.0
    )
    earlier = jnp.where(
        lax.broadcasted_iota(jnp.int32, (slots, 1), 0) < lax.broadcasted_iota(jnp.int32, (1, slots), 1),
        1.0, 0.0,
    )
    before = jnp.dot(
        bound.astype(jnp.bfloat16), earlier.astype(jnp.bfloat16), preferred_element_type=jnp.float32
    )
    position = jnp.sum(bound * before, axis=0, keepdims=True).astype(jnp.int32)
    place_row = jnp.where(away_row, facing * CAP + position, -1)
    row = lax.broadcasted_iota(jnp.int32, (sectors * SLAB, 1), 0)
    chunk = (row % SLAB) // CAP
    placed = place_row == (row // SLAB) * CAP + row % CAP
    wells = jnp.max(jnp.where(placed, well_row, -1), axis=1, keepdims=True)
    wells_out[...] = jnp.broadcast_to(wells, wells_out.shape)
    for q in range(TILES):
        placing[q] = jnp.where(placed & (chunk == q), 1.0, 0.0).astype(jnp.bfloat16)
    wells_in[slab(sector), :] = jnp.full((SLAB, 128), -1, jnp.int32)
    values_in[slab(sector), :] = jnp.zeros((SLAB, width), jnp.bfloat16)
    answers_in[slab(sector), :] = jnp.zeros((SLAB, width), jnp.bfloat16)

    def exchange(phase, source, dest):
        @pl.loop(1, sectors)
        def _(j):
            to_sector(
                phase, j, source.at[slab(lax.rem(sector + j, sectors)), :], dest.at[slab(sector), :]
            ).start()

    def arrived(phase, source, dest):
        @pl.loop(1, sectors)
        def _(j):
            to_sector(
                phase, j, source.at[slab(lax.rem(sector + j, sectors)), :],
                dest.at[slab(lax.rem(sector + sectors - j, sectors)), :],
            ).wait()

    exchange(0, wells_out, wells_in)

    def recv(phase, k, ref):
        to_tile(phase, k, ref, ref).wait_recv()

    per_tile = slots // BLK

    def expand(tile):
        names = cols_all[col_rows_of(tile), :]
        for inner in range(per_tile):
            rows = pl.ds(pl.multiple_of(tile * slots + inner * BLK, BLK), BLK)
            blocks = [coef[rows, n * BLK : (n + 1) * BLK].astype(jnp.float32) for n in range(NB)]
            for c in range(per_tile * TILES):
                value = jnp.zeros((BLK, BLK), jnp.float32)
                for n in range(NB):
                    name = names[inner * NB + n : inner * NB + n + 1, :]
                    value = jnp.where(name == c, blocks[n], value)
                dense[rows, c * BLK : (c + 1) * BLK] = value.astype(jnp.bfloat16)

    recv(1, 2, coef.at[slot_rows(peer[2]), :])
    send(1, 3, coef.at[slot_rows(peer[2]), :], coef.at[slot_rows(peer[2]), :], 1)
    arrived(0, wells_out, wells_in)
    match = (wells_in[:, 0:1] == well_row) & home_row
    for q in range(TILES):
        matching[q] = jnp.where(match & (chunk == q), 1.0, 0.0).astype(jnp.bfloat16)
    heard = lax.dot_general(
        matching[0], jnp.ones((sectors * SLAB, 128), jnp.bfloat16),
        (((0,), (0,)), ((), ())), preferred_element_type=jnp.float32,
    )
    scale = 1.0 / (2.0 + heard)
    roles_v[0] = scale
    kind = jnp.where(home_row, 2.0, jnp.where(shared_row, 1.0, 0.0))
    roles_v[1] = jnp.broadcast_to(kind, (128, slots)).T
    scale = scale[:, 0:1]
    outs = []

    def put(i, source, dest):
        copy = pltpu.make_async_copy(source, dest, out_sem.at[i])
        copy.start()
        outs.append(copy)

    put(4, placing, placing_o)
    put(5, matching, matching_o)
    put(6, roles_v, roles_o)

    for copy in loads[3:]:
        copy.wait()
    for k in (1, 2, 3):
        recv(0, k, cols_all.at[col_rows_of(peer[k]), :])
    expand(own)
    recv(1, 1, coef.at[slot_rows(peer[1]), :])
    expand(peer[1])
    expand(peer[2])
    recv(1, 3, coef.at[slot_rows(peer[3]), :])
    expand(peer[3])
    for k in (1, 2, 3):
        recv(2, k, start.at[slot_rows(peer[k]), :])

    part = 256

    def drawdown(at, source):
        rows = pl.ds(pl.multiple_of(at, part), part)
        return rows, jnp.dot(dense[rows, :], source[...], preferred_element_type=jnp.float32)

    def stepped(rows, source, drawn_rows):
        moved = source[rows, :].astype(jnp.float32) + pull[rows, :].astype(jnp.float32)
        return ((moved - 0.5 * drawn_rows) * (1.0 / 1.5)).astype(jnp.bfloat16)

    @pl.loop(0, slots * TILES // part)
    def _(block):
        rows, value = drawdown(block * part, start)
        drawn[rows, :] = value

    for k in (1, 2, 3):
        recv(3, k, pull.at[slot_rows(peer[k]), :])

    @pl.loop(0, per_tile * TILES)
    def _(block):
        rows = pl.ds(pl.multiple_of(block * BLK, BLK), BLK)
        state[0, rows, :] = stepped(rows, start, drawn[rows, :])

    for step in range(1, INNER - 1):
        source = state.at[(step + 1) % 2]
        dest = state.at[step % 2]

        @pl.loop(0, slots * TILES // part)
        def _(block):
            rows, value = drawdown(block * part, source)
            dest[rows, :] = stepped(rows, source, value)

    source = state.at[INNER % 2]
    for k in (2, 3, 1, 0):
        for inner in range(slots // part):
            rows, value = drawdown(peer[k] * slots + inner * part, source)
            result = stepped(rows, source, value)
            if k == 0:
                got_rates[own, inner * part : (inner + 1) * part, :] = result
            else:
                last[k, inner * part : (inner + 1) * part, :] = result
        if k > 0:
            send(4, k, last.at[k], got_rates.at[own])

    total = jnp.zeros((sectors * SLAB, width), jnp.float32)
    for k in range(TILES):
        q = peer[k]
        if k > 0:
            recv(4, k, got_rates.at[q])
        put(k, got_rates.at[q], rates_o.at[q])
        offer = (got_rates[q].astype(jnp.float32) + duals_v[:, share(q)]).astype(jnp.bfloat16)
        offered[k] = offer
        total += jnp.dot(placing[q], offer, preferred_element_type=jnp.float32)
    values_out[...] = total.astype(jnp.bfloat16)
    exchange(1, values_out, values_in)
    arrived(1, values_out, values_in)
    put(7, values_in, values_o)
    total = jnp.zeros((sectors * SLAB, width), jnp.float32)
    for k in range(TILES):
        q = peer[k]
        added = lax.dot_general(
            matching[q], values_in[...], (((0,), (0,)), ((), ())), preferred_element_type=jnp.float32
        )
        value = (2.0 * offered[k].astype(jnp.float32) + added) * scale
        total += jnp.dot(matching[q], value.astype(jnp.bfloat16), preferred_element_type=jnp.float32)
    answers_out[...] = total.astype(jnp.bfloat16)
    exchange(2, answers_out, answers_in)
    arrived(2, answers_out, answers_in)
    put(8, answers_in, answers_o)
    for copy in outs:
        copy.wait()
    for copy in sends:
        copy.wait_send()


def outputs_kernel(
    rates, duals, placing, matching, values, answers, roles, new_rates, new_duals, consensus
):
    ours = (((0,), (0,)), ((), ()))
    added = lax.dot_general(matching[0], values[...], ours, preferred_element_type=jnp.float32)
    from_peer = lax.dot_general(placing[0], answers[...], ours, preferred_element_type=jnp.float32)
    scale, kind = roles[0, :, 0:1], roles[1, :, 0:1]
    wide, kept = rates[0].astype(jnp.float32), duals[...]
    offer = (wide + kept).astype(jnp.bfloat16).astype(jnp.float32)
    mean = (2.0 * offer + added) * scale
    agreed = jnp.where(kind > 1.5, mean, jnp.where(kind > 0.5, from_peer, wide))
    new_rates[...] = rates[0]
    consensus[...] = agreed
    new_duals[...] = jnp.where(kind > 0.5, kept + wide - agreed, kept)


def shards(rates, target, prior_consensus, duals, response, block_cols, slot_well, well_owner):
    slots, periods = rates.shape
    sectors = lax.axis_size("sector")
    width = periods // TILES
    rows = TILES * slots
    slabs = sectors * SLAB
    cols = jnp.broadcast_to(block_cols.reshape(-1, 1), (block_cols.size, 128))
    bf16, f32, i32 = jnp.bfloat16, jnp.float32, jnp.int32
    whole = pl.BlockSpec(memory_space=pltpu.VMEM)
    far = pl.BlockSpec(memory_space=pl.ANY)
    dma = pltpu.SemaphoreType.DMA
    moved = pl.pallas_call(
        functools.partial(round_kernel, sectors),
        out_shape=(
            jax.ShapeDtypeStruct((TILES, slots, width), bf16),
            jax.ShapeDtypeStruct((TILES, slabs, slots), bf16),
            jax.ShapeDtypeStruct((TILES, slabs, slots), bf16),
            jax.ShapeDtypeStruct((slabs, width), bf16),
            jax.ShapeDtypeStruct((slabs, width), bf16),
            jax.ShapeDtypeStruct((2, slots, 128), f32),
        ),
        in_specs=[far] * 5 + [whole] * 3,
        out_specs=(far,) * 6,
        scratch_shapes=[
            pltpu.VMEM((rows, width), bf16),
            pltpu.VMEM((rows, width), bf16),
            pltpu.VMEM((TILES, slots, width), bf16),
            pltpu.VMEM((rows, NB * BLK), bf16),
            pltpu.VMEM((2, rows, width), bf16),
            pltpu.VMEM((TILES, slots, width), bf16),
            pltpu.VMEM((TILES, slots, width), bf16),
            pltpu.VMEM((rows, width), f32),
            pltpu.VMEM((rows, rows), bf16),
            pltpu.VMEM((TILES * block_cols.size, 128), i32),
            pltpu.VMEM((slots, periods), bf16),
            pltpu.VMEM((slots, periods), f32),
            pltpu.VMEM((slots, periods), f32),
            pltpu.VMEM((TILES, slabs, slots), bf16),
            pltpu.VMEM((TILES, slabs, slots), bf16),
            pltpu.VMEM((slabs, 128), i32),
            pltpu.VMEM((slabs, 128), i32),
            pltpu.VMEM((TILES, slots, width), bf16),
            pltpu.VMEM((slabs, width), bf16),
            pltpu.VMEM((slabs, width), bf16),
            pltpu.VMEM((slabs, width), bf16),
            pltpu.VMEM((slabs, width), bf16),
            pltpu.VMEM((2, slots, 128), f32),
            dma((5,)),
            dma((5, TILES)),
            dma((5, TILES)),
            dma((3, sectors)),
            dma((3, sectors)),
            dma((9,)),
        ],
        compiler_params=pltpu.CompilerParams(
            collective_id=0, has_side_effects=True, vmem_limit_bytes=56 << 20
        ),
    )(rates, target, prior_consensus, duals, response, cols, slot_well.reshape(1, -1), well_owner.reshape(1, -1))
    columns = pl.BlockSpec((slots, width), lambda q: (0, q))
    picks = pl.BlockSpec((1, slabs, slots), lambda q: (q, 0, 0))
    rows_sent = pl.BlockSpec((slabs, width), lambda q: (0, 0))
    return pl.pallas_call(
        outputs_kernel,
        grid=(TILES,),
        out_shape=(
            jax.ShapeDtypeStruct((slots, periods), bf16),
            jax.ShapeDtypeStruct((slots, periods), f32),
            jax.ShapeDtypeStruct((slots, periods), f32),
        ),
        in_specs=[
            pl.BlockSpec((1, slots, width), lambda q: (q, 0, 0)),
            columns, picks, picks, rows_sent, rows_sent,
            pl.BlockSpec((2, slots, 128), lambda q: (0, 0, 0)),
        ],
        out_specs=(columns, columns, columns),
        compiler_params=pltpu.CompilerParams(vmem_limit_bytes=(64 << 20) - (64 << 10)),
    )(moved[0], duals, *moved[1:])


def solution(mesh):
    both = P(("sector", "tile"), None)
    return jax.shard_map(
        shards,
        mesh=mesh,
        in_specs=(both, both, both, both, both, both, P(("sector", "tile")), P()),
        out_specs=(both, both, both),
        check_vma=False,
    )
```
